32 devices in a mesh: groups: 2 (over x), seq: 8 (over z, y), segment: 2 (over core).
Axes of the slice: x: 2, y: 2, z: 4, core: 2. Of those that a mesh axis runs over, the one named last changes fastest.
Arguments:
- queue_frames: bfloat16 [32, 32, 5120], P(('groups', 'segment'), 'seq'), parts along dimension 0, may hold values from -450 to 450
- fresh_frames: bfloat16 [2, 32, 5120], P('groups', 'seq'), parts along dimension 0, may hold values from -450 to 450
- slot_level: int32 [32], P(('groups', 'segment')), parts along dimension 0, may hold values from 0 to 49
- window_start: int32 [32], P(('groups', 'segment')), parts along dimension 0, may hold values from 0 to 3
- shift_table: float32 [50, 5120], replicated, may hold values from -3 to 3
- scale_table: float32 [50, 5120], replicated, may hold values from -1.5 to 1.5
- gate_table: float32 [50, 5120], replicated, may hold values from -10 to 10
- w_query: bfloat16 [5120, 4096], P(None, 'seq'), may hold values from -3.5 to 3.5
- w_key: bfloat16 [5120, 4096], P(None, 'seq'), may hold values from -3.5 to 3.5
- w_value: bfloat16 [5120, 4096], P(None, 'seq'), may hold values from -0.078125 to 0.078125
- w_out: bfloat16 [4096, 5120], P('seq'), may hold values from -0.5 to 0.5
- query_gain: float32 [4096], P('seq'), may hold values from 0.1 to 1.9
- key_gain: float32 [4096], P('seq'), may hold values from 0.1 to 1.9
Outputs:
- queue_out: bfloat16 [32, 32, 5120], P(('groups', 'segment'), 'seq'), parts along dimension 0
- departed: bfloat16 [4, 1, 32, 5120], P(('groups', 'segment'), None, 'seq'), parts along dimension 0
The draws below stay inside these ranges and needn't reach their ends.
There are 2 independent parts, one for each index of `groups`. The reference program is written for one: setup_inputs(seed, part) draws one part's arguments, and reference() takes and returns one part's arrays. A program takes and returns all parts, laid end to end along the dimension named above; an argument that names none is the same for every part. Nothing has to cross between parts.
All inputs are finite; a program needn't handle non-finite values.
Results may differ from the reference program's by a relative error of at most 0.02.
Values may be sent and summed in bfloat16 or wider, within the bound.
A program may use at most 128 MiB of HBM per device.

```python
import math
import jax
import jax.numpy as jnp
from jax import lax

D = 5120
HD = 128
HEADS = 32
FRAMES = 8
KEYWIN = 4
LEVELS = 50
STEPS = 1
FTOK = 32
QUEUE = 16
INNER = 4096
N_SEQ = 8


def noise_field(key, frame_count):
    normal_key, channel_key, token_key = jax.random.split(key, 3)
    shape_all = (frame_count, FTOK, D)
    log_span = math.log(10.0)
    noise_rows = jnp.clip(jax.random.normal(normal_key, shape_all), -6.0, 6.0)
    ramp = jnp.arange(D, dtype=jnp.float32) / max(D - 1, 1)
    ramp_scale = jnp.exp(log_span * (ramp - 0.5))
    channel_scale = jnp.exp(jax.random.uniform(channel_key, (D,), minval=-0.7, maxval=0.7))
    token_scale = jnp.exp(jax.random.uniform(token_key, (frame_count, FTOK), minval=-0.5 * math.log(10.0), maxval=0.5 * math.log(10.0)))
    return noise_rows * (ramp_scale * channel_scale)[None, None, :] * token_scale[:, :, None]


def draw_queue_frames(key, part):
    noise_rows = noise_field(jax.random.fold_in(key, 11), QUEUE)
    return noise_rows.astype(jnp.bfloat16)


def draw_fresh_frames(key, part):
    return noise_field(jax.random.fold_in(key, 21), STEPS).astype(jnp.bfloat16)


def dense_weight(key, salt):
    inner_width = HEADS * HD
    base = jnp.clip(jax.random.normal(jax.random.fold_in(key, salt), (D, inner_width)), -6.0, 6.0)
    column_span = math.log(6.0)
    column_pos = jnp.arange(inner_width, dtype=jnp.float32) / max(inner_width - 1, 1)
    column_scale = jnp.exp(column_span * (column_pos - 0.5))
    return base * D ** (-0.5) * column_scale[None, :]


def draw_w_query(key, part):
    weight_rows = dense_weight(key, 31)
    return weight_rows.astype(jnp.bfloat16)


def draw_w_key(key, part):
    weight_rows = dense_weight(key, 41)
    return weight_rows.astype(jnp.bfloat16)


def touch_ends(values, own_key, smallest, top_value):
    spot = [jax.random.randint(jax.random.fold_in(own_key, axis), (), 0, length) for axis, length in enumerate(values.shape)]
    longest = values.shape.index(max(values.shape))
    next_to = spot[:longest] + [(spot[longest] + 1) % values.shape[longest]] + spot[longest + 1:]
    return values.at[tuple(spot)].set(smallest).at[tuple(next_to)].set(top_value)


def shard_levels(own_key, dims, cuts, smallest, top_value):
    loudness = 1.0
    for position, shards_of in cuts:
        steps = jax.random.uniform(jax.random.fold_in(jax.random.fold_in(own_key, 6), position), (shards_of,), jnp.float32, smallest / len(cuts), top_value / len(cuts))
        loudness = loudness * jnp.repeat(jnp.exp(steps), dims[position] // shards_of).reshape((-1,) + (1,) * (len(dims) - 1 - position))
    return loudness


def centred(rng, dims, scale, limit, shards=(), kind=jnp.bfloat16):
    drawn = scale * jax.random.normal(rng, dims, jnp.float32)
    if shards:
        drawn = drawn * shard_levels(rng, dims, shards, -0.22, 0.18)
    return jnp.clip(drawn, -limit, limit).astype(kind)


def setup_inputs(seed: int = 0, part: int = 0) -> dict:
    seeds = jax.random.split(jax.random.key(seed), 14)
    part_splits = jax.random.split(jax.random.fold_in(seeds[13], part), 14)
    queue_frames = draw_queue_frames(jax.random.fold_in(jax.random.fold_in(seeds[13], part), 71), part)
    fresh_frames = draw_fresh_frames(jax.random.fold_in(jax.random.fold_in(seeds[13], part), 71), part)
    slot_level = touch_ends(jax.random.randint(part_splits[2], (QUEUE,), 0, LEVELS), jax.random.fold_in(part_splits[2], 1), 0, LEVELS - 1).astype(jnp.int32)
    window_start = touch_ends(jax.random.randint(part_splits[3], (QUEUE,), 0, KEYWIN), jax.random.fold_in(part_splits[3], 1), 0, KEYWIN - 1).astype(jnp.int32)
    shift_table = centred(seeds[4], (LEVELS, D), 0.5, 3.0, (), jnp.float32)
    scale_table = centred(seeds[5], (LEVELS, D), 0.3, 1.5, (), jnp.float32)
    gate_table = centred(seeds[6], (LEVELS, D), 2.0, 10.0, (), jnp.float32)
    w_query = draw_w_query(jax.random.fold_in(seeds[13], 71), part)
    w_key = draw_w_key(jax.random.fold_in(seeds[13], 71), part)
    w_value = centred(seeds[9], (D, INNER), D ** -0.5, 0.078125, ((1, 8),))
    w_out = centred(seeds[10], (INNER, D), HD ** -0.5, 0.5, ((0, 8),))
    query_gain = jnp.clip(1.0 + 0.18 * jax.random.normal(seeds[11], (INNER,), jnp.float32), 0.1, 1.9)
    key_gain = jnp.clip(1.0 + 0.18 * jax.random.normal(seeds[12], (INNER,), jnp.float32), 0.1, 1.9)
    return dict(queue_frames=queue_frames, fresh_frames=fresh_frames, slot_level=slot_level, window_start=window_start, shift_table=shift_table, scale_table=scale_table, gate_table=gate_table, w_query=w_query, w_key=w_key, w_value=w_value, w_out=w_out, query_gain=query_gain, key_gain=key_gain)


epsilon = 1e-06
masked_score = -1e+30

def modulate(level_ids, lookup):
    onehot = (level_ids[:, None] == jnp.arange(lookup.shape[0], dtype=jnp.int32)[None, :]).astype(jnp.float32)
    return jnp.dot(onehot, lookup, precision=lax.Precision.HIGHEST)

def head_norm(raw, gain):
    inverse = lax.rsqrt(lax.optimization_barrier(jnp.mean(raw * raw, axis=1, keepdims=True)) + epsilon)
    return (raw * inverse * gain[None, :]).astype(jnp.bfloat16)

def attend_block(queries, key_rows, value_rows, usable):
    scores = jnp.einsum('qhd,khd->hqk', queries.astype(jnp.float32), key_rows.astype(jnp.float32)) * HD ** (-0.5)
    scores = jnp.where(usable[None, None, :], scores, masked_score)
    largest = lax.optimization_barrier(jnp.max(scores, axis=2, keepdims=True))
    lifted = jnp.exp(scores - largest)
    totals = lax.optimization_barrier(jnp.sum(lifted, axis=2, keepdims=True))
    weights = (lifted / totals).astype(jnp.bfloat16)
    return jnp.einsum('hqk,khd->qhd', weights.astype(jnp.float32), value_rows.astype(jnp.float32)).astype(jnp.bfloat16)

def layer_step(queue_state, slot_level, window_start, shift_table, scale_table, gate_table, w_query, w_key, w_value, w_out, query_gain, key_gain):
    queue_len = queue_state.shape[0]
    token_count = queue_state.shape[1]
    width = queue_state.shape[2]
    values_in = queue_state.astype(jnp.float32)
    inverse = lax.rsqrt(lax.optimization_barrier(jnp.mean(values_in * values_in, axis=2)) + epsilon)
    shift_rows = modulate(slot_level, shift_table)
    scale_rows = modulate(slot_level, scale_table)
    gate_rows = modulate(slot_level, gate_table)
    hidden = (values_in * inverse[:, :, None] * (1.0 + scale_rows[:, None]) + shift_rows[:, None]).astype(jnp.bfloat16)
    flat = hidden.reshape(queue_len * token_count, width)
    q_raw = jnp.dot(flat, w_query, preferred_element_type=jnp.float32)
    k_raw = jnp.dot(flat, w_key, preferred_element_type=jnp.float32)
    value_all = jnp.dot(flat, w_value, preferred_element_type=jnp.float32).astype(jnp.bfloat16)
    queries = head_norm(q_raw, query_gain).reshape(queue_len, token_count, HEADS, HD)
    key_all = head_norm(k_raw, key_gain).reshape(queue_len, token_count, HEADS, HD)
    value_all = value_all.reshape(queue_len, token_count, HEADS, HD)
    rim_width = KEYWIN - 1
    padding = ((rim_width, rim_width), (0, 0), (0, 0), (0, 0))
    key_pad = jnp.pad(key_all, padding)
    value_pad = jnp.pad(value_all, padding)

    def one_frame(frame_idx):
        window_begin = (frame_idx - window_start[frame_idx] + rim_width).astype(jnp.int32)
        key_rows = lax.dynamic_slice_in_dim(key_pad, window_begin, KEYWIN, 0).reshape(KEYWIN * token_count, HEADS, HD)
        value_rows = lax.dynamic_slice_in_dim(value_pad, window_begin, KEYWIN, 0).reshape(KEYWIN * token_count, HEADS, HD)
        frame_ids = window_begin - rim_width + jnp.arange(KEYWIN, dtype=jnp.int32)
        usable = jnp.repeat((frame_ids >= 0) & (frame_ids < queue_len), token_count)
        return attend_block(queries[frame_idx], key_rows, value_rows, usable)
    attended = lax.map(one_frame, jnp.arange(queue_len, dtype=jnp.int32))
    group_width = HEADS // N_SEQ * HD
    grouped = jnp.transpose(attended.reshape(queue_len * token_count, N_SEQ, group_width), (1, 0, 2))
    weight_groups = w_out.reshape(N_SEQ, group_width, width)

    def add_group(total, pair):
        rows, weight_rows = pair
        partial_value = jnp.dot(rows, weight_rows, preferred_element_type=jnp.float32).astype(jnp.bfloat16)
        partial_value = lax.optimization_barrier(partial_value)
        return (total + partial_value.astype(jnp.float32), None)
    start_total = jnp.zeros((queue_len * token_count, width), jnp.float32)
    projected, unused = lax.scan(add_group, start_total, (grouped, weight_groups))
    projected = projected.reshape(queue_len, token_count, width)
    return (values_in + gate_rows[:, None] * projected).astype(jnp.bfloat16)

def reference(queue_frames, fresh_frames, slot_level, window_start, shift_table, scale_table, gate_table, w_query, w_key, w_value, w_out, query_gain, key_gain):
    queue_state = queue_frames
    departed = []
    for step_idx in range(STEPS):
        updated = layer_step(queue_state, slot_level, window_start, shift_table, scale_table, gate_table, w_query, w_key, w_value, w_out, query_gain, key_gain)
        departed.append(updated[::FRAMES])
        queue_state = jnp.concatenate([updated[1:], fresh_frames[step_idx][None]], axis=0)
    return (queue_state, jnp.stack(departed, axis=1))
```

```python
import functools

import jax
import jax.numpy as jnp
from jax import lax
from jax.experimental import pallas as pl
from jax.experimental.pallas import tpu as pltpu
from jax.sharding import PartitionSpec as P

HD = 128
KEYWIN = 4
epsilon = 1e-06
masked_score = -1e30
MESH = pl.DeviceIdType.MESH
F32 = jnp.float32
BF16 = jnp.bfloat16
NT = (((1,), (1,)), ((), ()))


def quotient(x, n):
    return x >> (n.bit_length() - 1) if n & (n - 1) == 0 else x // n


def remainder(x, n):
    return x & (n - 1) if n & (n - 1) == 0 else x % n


def chunk_count(width):
    lanes = width // 128
    return max(k for k in range(1, 9) if lanes % k == 0)


def kernel(
    n, frames, tok, parts,
    x_ref, fresh_ref, level_ref, start_ref, shift_hbm, scale_hbm, gate_hbm,
    wq_hbm, wk_hbm, wv_hbm, wo_hbm, qgain_ref, kgain_ref,
    queue_ref, departed_ref,
    shift_rows, scale_rows, gate_rows, w_in, w_out, hidden, gathered, raw, stats, keys, vals, att,
    partial, from_y, from_up, from_down, projected, hand,
    local_sem, wo_sem, ag_send, ag_recv, st_send, st_recv, kv_send, kv_recv,
    y_send, y_recv, z_send, up_recv, down_recv, hand_send, hand_recv,
):
    me = lax.axis_index("seq")
    seg = lax.axis_index("segment")
    other = 1 - seg
    nz = n // 2
    z, y = quotient(me, 2), remainder(me, 2)
    block = frames * tok
    rows = n * block
    width = x_ref.shape[2]
    cw = width // parts
    lw = qgain_ref.shape[1]
    heads = lw // HD

    def local(k, src, dst):
        return pltpu.make_async_copy(src, dst, local_sem.at[k])

    locals_ = [
        local(0, shift_hbm, shift_rows),
        local(1, scale_hbm, scale_rows),
        local(2, wq_hbm, w_in.at[:, pl.ds(0, lw)]),
        local(3, wk_hbm, w_in.at[:, pl.ds(lw, lw)]),
        local(4, wv_hbm, w_in.at[:, pl.ds(2 * lw, lw)]),
        local(5, gate_hbm, gate_rows),
    ]
    wo_copies = [
        pltpu.make_async_copy(wo_hbm.at[:, pl.ds(c * cw, cw)], w_out.at[c], wo_sem.at[c])
        for c in range(parts)
    ]
    for copy in locals_ + wo_copies:
        copy.start()

    def remote(src, dst, send, recv, s, g):
        return pltpu.make_async_remote_copy(
            src_ref=src, dst_ref=dst, send_sem=send, recv_sem=recv,
            device_id={"seq": s, "segment": g}, device_id_type=MESH,
        )

    barrier = pltpu.get_barrier_semaphore()

    @pl.loop(1, 2 * n)
    def _(k):
        peer = remainder(me * 2 + seg + k, 2 * n)
        pl.semaphore_signal(
            barrier, inc=1,
            device_id={"seq": quotient(peer, 2), "segment": remainder(peer, 2)},
            device_id_type=MESH,
        )

    locals_[0].wait()
    locals_[1].wait()
    for f in range(frames):
        level = level_ref[f]
        x = x_ref[f].astype(F32)
        inverse = lax.rsqrt(jnp.mean(x * x, axis=1, keepdims=True) + epsilon)
        scale = scale_rows[pl.ds(level, 1), :]
        shift = shift_rows[pl.ds(level, 1), :]
        hidden[pl.ds(f * tok, tok), :] = x * inverse * (1.0 + scale) + shift
    for c in range(parts):
        gathered[c, me] = hidden[:, c * cw : (c + 1) * cw].astype(BF16)
    raw[...] = jnp.zeros_like(raw)
    hand[...] = jnp.zeros_like(hand)
    pl.semaphore_wait(barrier, 2 * n - 1)

    def ag_copy(c, zb, yb, kind, to):
        ref = gathered.at[c, zb * 2 + yb]
        return remote(ref, ref, ag_send.at[c, zb, kind], ag_recv.at[c, zb * 2 + yb], to, seg)

    def ag_forward(d, c, act):
        up, down = z - d, z + d
        if d > 0:
            @pl.when(up >= 0)
            def _():
                if act == "start":
                    ag_copy(c, up, y, 2, me).wait_recv()
                move(ag_copy(c, up, y, 2, z * 2 + 1 - y), act)

        @pl.when((up >= 0) & (z + 1 < nz))
        def _():
            move(ag_copy(c, up, y, 0, me + 2), act)

        @pl.when(down < nz)
        def _():
            if d > 0 and act == "start":
                ag_copy(c, down, y, 2, me).wait_recv()
            move(ag_copy(c, down, y, 2, z * 2 + 1 - y), act)

        @pl.when((down < nz) & (z > 0))
        def _():
            move(ag_copy(c, down, y, 1, me - 2), act)

    def move(copy, act):
        if act == "start":
            copy.start()
        else:
            copy.wait_send()

    for d in range(nz - 1):
        @pl.loop(0, parts)
        def _(c):
            ag_forward(d, c, "start")

    for copy in locals_[2:5]:
        copy.wait()

    @pl.loop(0, parts + 1)
    def _(t):
        @pl.when(t < parts)
        def _():
            ag_forward(nz - 1, t, "start")

        @pl.when(t > 0)
        def _():
            c = t - 1

            @pl.loop(0, nz)
            def _(zb):
                ag_copy(c, zb, 1 - y, 2, me).wait_recv()

            at = pl.multiple_of(c * cw, cw)
            raw[...] += jnp.dot(
                gathered[c].reshape(rows, cw), w_in[pl.ds(at, cw), :],
                preferred_element_type=F32,
            )

    ones = jnp.ones((8, lw), F32)
    q_raw = raw[:, :lw]
    k_raw = raw[:, lw : 2 * lw]
    q_sq = lax.dot_general(ones, q_raw * q_raw, NT, precision=lax.Precision.HIGHEST,
                           preferred_element_type=F32)
    k_sq = lax.dot_general(ones, k_raw * k_raw, NT, precision=lax.Precision.HIGHEST,
                           preferred_element_type=F32)
    row_id = lax.broadcasted_iota(jnp.int32, (8, rows), 0)
    stats[seg, me] = jnp.where(row_id == 0, q_sq, k_sq)

    def st_copy(slot, to):
        s, g = quotient(to, 2), remainder(to, 2)
        ref = stats.at[seg, me]
        return remote(ref, ref, st_send.at[slot], st_recv.at[seg, me], s, g)

    @pl.loop(1, 2 * n)
    def _(k):
        st_copy(k, remainder(me * 2 + seg + k, 2 * n)).start()

    keys[seg] = (k_raw * kgain_ref[...]).astype(BF16)
    vals[seg] = raw[:, 2 * lw :].astype(BF16)
    k_copy = remote(keys.at[seg], keys.at[seg], kv_send.at[0], kv_recv.at[0], me, other)
    v_copy = remote(vals.at[seg], vals.at[seg], kv_send.at[1], kv_recv.at[1], me, other)
    k_copy.start()
    v_copy.start()

    for d in range(nz):
        @pl.loop(0, parts)
        def _(c):
            ag_forward(d, c, "drain")

    @pl.loop(1, 2 * n)
    def _(k):
        peer = remainder(me * 2 + seg + k, 2 * n)
        ref = stats.at[remainder(peer, 2), quotient(peer, 2)]
        remote(ref, ref, st_send.at[k],
               st_recv.at[remainder(peer, 2), quotient(peer, 2)], me, other).wait_recv()

    inner = n * lw
    totals = lax.rsqrt(jnp.sum(stats[...], axis=1) / inner + epsilon)
    own_totals = jnp.where(seg == 0, totals[0], totals[1])
    q_inverse = jnp.transpose(own_totals)[:, 0:1]
    queries = (raw[:, :lw] * q_inverse * qgain_ref[...]).astype(BF16)
    raw[:, :lw] = queries.astype(F32)
    k_inverse = jnp.concatenate([totals[0, 1:2], totals[1, 1:2]], axis=1) * HD ** (-0.5)
    k_copy.wait_recv()
    v_copy.wait_recv()

    qb = min(rows, 256)
    key_id = lax.broadcasted_iota(jnp.int32, (qb, 2 * rows), 1)
    key_frame = quotient(key_id, rows) * frames + quotient(remainder(key_id, block), tok)
    query_id = lax.broadcasted_iota(jnp.int32, (qb, 1), 0)
    query_frame = quotient(remainder(query_id, block), tok)
    begin = jnp.zeros((qb, 1), jnp.int32)
    for f in range(frames):
        begin = jnp.where(query_frame == f, seg * frames + f - start_ref[f], begin)
    usable = (key_frame >= begin) & (key_frame < begin + KEYWIN)

    @pl.loop(0, rows // qb)
    def _(b):
        at = pl.ds(pl.multiple_of(b * qb, qb), qb)
        for h in range(heads):
            lanes = slice(h * HD, (h + 1) * HD)
            head_keys = keys[:, :, lanes].reshape(2 * rows, HD)
            head_vals = vals[:, :, lanes].reshape(2 * rows, HD)
            scores = lax.dot_general(raw[at, lanes].astype(BF16), head_keys, NT,
                                     preferred_element_type=F32) * k_inverse
            scores = jnp.where(usable, scores, masked_score)
            lifted = jnp.exp(scores - jnp.max(scores, axis=1, keepdims=True))
            weights = (lifted / jnp.sum(lifted, axis=1, keepdims=True)).astype(BF16)
            att[at, lanes] = jnp.dot(weights, head_vals, preferred_element_type=F32).astype(BF16)

    def y_copy(c):
        return remote(partial.at[c, 1 - y], from_y.at[c], y_send.at[c], y_recv.at[c],
                      z * 2 + 1 - y, seg)

    for c in range(parts):
        wo_copies[c].wait()
        product = jnp.dot(att[...], w_out[c], preferred_element_type=F32).astype(BF16)
        product = product.reshape(nz, 2, block, cw)
        partial[c, 0] = product[:, 0]
        partial[c, 1] = product[:, 1]
        y_copy(c).start()

    def up_copy(c, zb):
        return remote(partial.at[c, y, zb], from_up.at[c, zb], z_send.at[c, zb],
                      up_recv.at[c, zb], me + 2, seg)

    def down_copy(c, zb):
        return remote(partial.at[c, y, zb], from_down.at[c, zb], z_send.at[c, zb],
                      down_recv.at[c, zb], me - 2, seg)

    def add(c, zb, other_ref):
        total = partial[c, y, zb].astype(F32) + other_ref[c, zb].astype(F32)
        partial[c, y, zb] = total.astype(BF16)

    @pl.loop(0, parts + nz - 1)
    def _(t):
        @pl.when(t < parts)
        def _():
            y_copy(t).wait_recv()

            @pl.loop(0, nz)
            def _(zb):
                add(t, zb, from_y)

        up, down = t - z, t - (nz - 1 - z)

        @pl.when((up >= 0) & (up < parts) & (z + 1 < nz))
        def _():
            @pl.loop(z + 1, nz)
            def _(zb):
                @pl.when(z > 0)
                def _():
                    up_copy(up, zb).wait_recv()
                    add(up, zb, from_up)

                up_copy(up, zb).start()

        @pl.when((down >= 0) & (down < parts) & (z > 0))
        def _():
            @pl.loop(0, z)
            def _(zb):
                @pl.when(z + 1 < nz)
                def _():
                    down_copy(down, zb).wait_recv()
                    add(down, zb, from_down)

                down_copy(down, zb).start()

        @pl.when(t >= nz - 1)
        def _():
            c = t - (nz - 1)
            projected[c] = partial[c, y, z].astype(F32)

            @pl.when(z > 0)
            def _():
                up_copy(c, z).wait_recv()
                projected[c] += from_up[c, z].astype(F32)

            @pl.when(z + 1 < nz)
            def _():
                down_copy(c, z).wait_recv()
                projected[c] += from_down[c, z].astype(F32)

    locals_[5].wait()
    hand_copy = remote(hand.at[0], hand.at[1], hand_send, hand_recv, me, 0)
    for f in range(frames):
        gate = gate_rows[pl.ds(level_ref[f], 1), :]
        for c in range(parts):
            lanes = slice(c * cw, (c + 1) * cw)
            updated = x_ref[f, :, lanes].astype(F32) + (
                gate[:, lanes] * projected[c, f * tok : (f + 1) * tok, :]
            )
            updated = updated.astype(BF16)
            if f == 0:
                departed_ref[0, 0, :, lanes] = updated
                hand[0, 0:tok, lanes] = updated
            else:
                queue_ref[f - 1, :, lanes] = updated
        if f == 0:
            @pl.when(seg == 1)
            def _():
                hand_copy.start()

    @pl.loop(0, parts)
    def _(c):
        y_copy(c).wait_send()

        @pl.loop(z + 1, nz)
        def _(zb):
            up_copy(c, zb).wait_send()

        @pl.loop(0, z)
        def _(zb):
            down_copy(c, zb).wait_send()

    @pl.loop(1, 2 * n)
    def _(k):
        st_copy(k, remainder(me * 2 + seg + k, 2 * n)).wait_send()

    k_copy.wait_send()
    v_copy.wait_send()

    @pl.when(seg == 1)
    def _():
        queue_ref[frames - 1] = fresh_ref[0]
        hand_copy.wait_send()

    @pl.when(seg == 0)
    def _():
        hand_copy.wait_recv()
        queue_ref[frames - 1] = hand[1, 0:tok, :]


def shards(
    n, queue_frames, fresh_frames, slot_level, window_start, shift_table, scale_table, gate_table,
    w_query, w_key, w_value, w_out, query_gain, key_gain,
):
    frames, tok, width = queue_frames.shape
    parts = chunk_count(width)
    cw = width // parts
    block = frames * tok
    rows = n * block
    lw = w_query.shape[1]
    nz = n // 2
    levels = shift_table.shape[0]
    vmem = pl.BlockSpec(memory_space=pltpu.VMEM)
    smem = pl.BlockSpec(memory_space=pltpu.SMEM)
    hbm = pl.BlockSpec(memory_space=pl.ANY)
    dma = pltpu.SemaphoreType.DMA
    scratch = [
        pltpu.VMEM((levels, width), F32),
        pltpu.VMEM((levels, width), F32),
        pltpu.VMEM((levels, width), F32),
        pltpu.VMEM((width, 3 * lw), BF16),
        pltpu.VMEM((parts, lw, cw), BF16),
        pltpu.VMEM((block, width), F32),
        pltpu.VMEM((parts, n, block, cw), BF16),
        pltpu.VMEM((rows, 3 * lw), F32),
        pltpu.VMEM((2, n, 8, rows), F32),
        pltpu.VMEM((2, rows, lw), BF16),
        pltpu.VMEM((2, rows, lw), BF16),
        pltpu.VMEM((rows, lw), BF16),
        pltpu.VMEM((parts, 2, nz, block, cw), BF16),
        pltpu.VMEM((parts, nz, block, cw), BF16),
        pltpu.VMEM((parts, nz, block, cw), BF16),
        pltpu.VMEM((parts, nz, block, cw), BF16),
        pltpu.VMEM((parts, block, cw), F32),
        pltpu.VMEM((2, 16, width), BF16),
        dma((6,)),
        dma((parts,)),
        dma((parts, nz, 3)),
        dma((parts, n)),
        dma((2 * n,)),
        dma((2, n)),
        dma((2,)),
        dma((2,)),
        dma((parts,)),
        dma((parts,)),
        dma((parts, nz)),
        dma((parts, nz)),
        dma((parts, nz)),
        dma,
        dma,
    ]
    return pl.pallas_call(
        functools.partial(kernel, n, frames, tok, parts),
        out_shape=(
            jax.ShapeDtypeStruct((frames, tok, width), BF16),
            jax.ShapeDtypeStruct((1, 1, tok, width), BF16),
        ),
        in_specs=[vmem, vmem, smem, smem] + [hbm] * 7 + [vmem, vmem],
        out_specs=(vmem, vmem),
        scratch_shapes=scratch,
        compiler_params=pltpu.CompilerParams(
            collective_id=0, has_side_effects=True, vmem_limit_bytes=60 * 1024 * 1024
        ),
    )(
        queue_frames, fresh_frames, slot_level, window_start, shift_table, scale_table, gate_table,
        w_query, w_key, w_value, w_out, query_gain[None], key_gain[None],
    )


def solution(mesh):
    n = mesh.shape["seq"]
    assert n % 2 == 0 and mesh.shape["segment"] == 2
    return jax.shard_map(
        functools.partial(shards, n),
        mesh=mesh,
        in_specs=(
            P(("groups", "segment"), "seq", None),
            P("groups", "seq", None),
            P(("groups", "segment")),
            P(("groups", "segment")),
            P(),
            P(),
            P(),
            P(None, "seq"),
            P(None, "seq"),
            P(None, "seq"),
            P("seq", None),
            P("seq"),
            P("seq"),
        ),
        out_specs=(
            P(("groups", "segment"), "seq", None),
            P(("groups", "segment"), None, "seq", None),
        ),
        check_vma=False,
    )
```
